256 devices in a mesh: row: 4 (over x), col: 4 (over z_lo, core), dp: 16 (over z_hi, y).
Axes of the slice: x: 4, y: 4, z: 8 (z_hi: 4, z_lo: 2; z = z_hi * 2 + z_lo), core: 2. Of those that a mesh axis runs over, the one named last changes fastest.
Arguments:
- tokens: bfloat16 [512, 5120], P(('col', 'dp'), 'row'), may hold values from -6 to 6
- w_gate_up: bfloat16 [2, 27648, 5120], P(None, ('col', 'dp'), 'row'), may hold values from -0.078125 to 0.078125
- w_down: bfloat16 [27648, 5120], P(('col', 'dp'), 'row'), may hold values from -0.0390625 to 0.0390625
- cotangent: bfloat16 [512, 5120], P(('col', 'dp'), 'row'), may hold values from -6 to 6
Outputs:
- output: bfloat16 [512, 5120], P(('col', 'dp'), 'row')
- d_tokens: bfloat16 [512, 5120], P(('col', 'dp'), 'row')
- d_gate_up: bfloat16 [2, 27648, 5120], P(None, ('col', 'dp'), 'row')
- d_down: bfloat16 [27648, 5120], P(('col', 'dp'), 'row')
The draws below stay inside these ranges and needn't reach their ends.
All inputs are finite; a program needn't handle non-finite values.
Results may differ from the reference program's by a relative error of at most 0.005.
Values may be sent and summed in bfloat16 or wider, within the bound.
A program may use at most 64 MiB of HBM per device.

```python
import jax
import jax.numpy as jnp

D = 5120
FF = 27648
TOKENS = 512


def block_scale(rng, dims, split, smallest, high):
    level = 1.0
    for axis_at, blocks in split:
        heights = jax.random.uniform(jax.random.fold_in(jax.random.fold_in(rng, 6), axis_at), (blocks,), jnp.float32, smallest / len(split), high / len(split))
        level = level * jnp.repeat(jnp.exp(heights), dims[axis_at] // blocks).reshape((-1,) + (1,) * (len(dims) - 1 - axis_at))
    return level


def normal_values(stream_key, extent, deviation, bound, cuts=(), dtype=jnp.bfloat16):
    level = block_scale(stream_key, extent, cuts, -0.22, 0.18) if cuts else 1.0
    result = jax.random.normal(stream_key, extent, jnp.float32) * deviation * level
    return jnp.minimum(jnp.maximum(result, -bound), bound).astype(dtype)


def setup_inputs(seed: int = 0) -> dict:
    arg_keys = jax.random.split(jax.random.key(seed), 5)
    return {
        "tokens": normal_values(arg_keys[0], (TOKENS, D), 1.0, 6.0, ((0, 64), (1, 4))),
        "w_gate_up": normal_values(arg_keys[1], (2, FF, D), D ** -0.5, 0.078125, ((1, 64), (2, 4))),
        "w_down": normal_values(arg_keys[2], (FF, D), FF ** -0.5, 0.0390625, ((0, 64), (1, 4))),
        "cotangent": normal_values(arg_keys[3], (TOKENS, D), 1.0, 6.0, ((0, 64), (1, 4))),
    }


def reference(tokens, w_gate_up, w_down, cotangent):
    gate = jnp.dot(tokens, w_gate_up[0].T, preferred_element_type=jnp.float32)
    up = jnp.dot(tokens, w_gate_up[1].T, preferred_element_type=jnp.float32)
    sig = jax.nn.sigmoid(gate)
    act = gate * sig
    hidden = (act * up).astype(jnp.bfloat16)
    output = jnp.dot(hidden, w_down, preferred_element_type=jnp.float32).astype(jnp.bfloat16)
    slope = jnp.dot(cotangent, w_down.T, preferred_element_type=jnp.float32)
    g_up = (slope * act).astype(jnp.bfloat16)
    g_gate = (slope * up * sig * (1.0 + gate * (1.0 - sig))).astype(jnp.bfloat16)
    d_tokens = jnp.dot(g_gate, w_gate_up[0], preferred_element_type=jnp.float32)
    d_tokens = d_tokens + jnp.dot(g_up, w_gate_up[1], preferred_element_type=jnp.float32)
    d_tokens = d_tokens.astype(jnp.bfloat16)
    d_gate = jnp.dot(g_gate.T, tokens, preferred_element_type=jnp.float32)
    d_upper = jnp.dot(g_up.T, tokens, preferred_element_type=jnp.float32)
    d_gate_up = jnp.stack([d_gate, d_upper]).astype(jnp.bfloat16)
    d_down = jnp.dot(hidden.T, cotangent, preferred_element_type=jnp.float32).astype(jnp.bfloat16)
    return (output, d_tokens, d_gate_up, d_down)
```

```python
import jax
import jax.numpy as jnp
from jax import lax
from jax.experimental import pallas as pl
from jax.experimental.pallas import tpu as pltpu
from jax.sharding import PartitionSpec as P

NX, NY, NZ = 4, 4, 8
CHIPS = NY * NZ
CHUNKS = 4
PER = CHIPS // CHUNKS
ROWS = 16
CT = PER * ROWS
ZTABLE = sum(d << (3 * i) for i, d in enumerate((1, 7, 6, 3, 5, 4, 2, 0)))
BF = jnp.bfloat16
F32 = jnp.float32
MESH = pl.DeviceIdType.MESH


def kernel(tok_ref, cot_ref, wgu_hbm, wd_hbm, out_ref, dtok_ref, dgu_hbm, dd_hbm,
           w, wout, tc, xf, ps, pr, pf, hid, part, pex, rs, rr, acc, fx,
           w_sem, o_sem, xf_sem, ag_send, ag_recv, fw_send, fw_recv,
           xr_send, xr_recv, xa_send, xa_recv, pe_send, pe_recv,
           rs_send, rs_recv, fx_sem):
    x = lax.axis_index("row")
    col = lax.axis_index("col")
    dp = lax.axis_index("dp")
    k = col % 2
    y = dp % 4
    z = (dp // 4) * 2 + col // 2
    ff = wd_hbm.shape[0]
    fpad = w.shape[1]
    fx_rows = fpad // NX

    def chip(dy, dz):
        yy = (y + dy) % NY
        zz = (z + dz) % NZ
        return (x, (zz % 2) * 2 + k, (zz // 2) * 4 + yy)

    def offsets(s):
        dz = lax.shift_right_logical(jnp.int32(ZTABLE), 3 * (s // 4)) % 8
        return 3 - s % 4, dz

    partner = (x, col + 1 - 2 * k, dp)

    def xpeer(r):
        return ((x + r) % NX, col, dp)

    loads = [
        pltpu.make_async_copy(wgu_hbm.at[0], w.at[0, pl.ds(0, ff)], w_sem.at[0]),
        pltpu.make_async_copy(wgu_hbm.at[1], w.at[1, pl.ds(0, ff)], w_sem.at[1]),
        pltpu.make_async_copy(wd_hbm, w.at[2, pl.ds(0, ff)], w_sem.at[2]),
    ]
    for c in loads:
        c.start()

    bar = pltpu.get_barrier_semaphore()
    pl.semaphore_signal(bar, inc=1, device_id=partner, device_id_type=MESH)

    @pl.loop(0, CHIPS - 1)
    def _(s):
        dy, dz = offsets(s)
        pl.semaphore_signal(bar, inc=1, device_id=chip(dy, dz), device_id_type=MESH)

    @pl.loop(1, NX)
    def _(r):
        pl.semaphore_signal(bar, inc=1, device_id=xpeer(r), device_id_type=MESH)

    first = k == 0
    tok = tok_ref[...].astype(F32)
    cot = cot_ref[...].astype(F32)
    keep = jnp.where(first, tok, cot)
    xf[0] = jnp.where(first, cot, tok)
    if fpad > ff:
        w[:, pl.ds(ff, fpad - ff), :] = jnp.zeros((3, fpad - ff, w.shape[2]), BF)
    pl.semaphore_wait(bar, 1 + (CHIPS - 1) + (NX - 1))

    swap = pltpu.make_async_remote_copy(
        src_ref=xf.at[0], dst_ref=xf.at[1], send_sem=xf_sem.at[0], recv_sem=xf_sem.at[1],
        device_id=partner, device_id_type=MESH)
    swap.start()
    swap.wait()
    got = xf[1]
    own = jnp.concatenate([jnp.where(first, keep, got), jnp.where(first, got, keep)], axis=0)
    tc[k, CHIPS - 1] = own.astype(BF)

    @pl.loop(0, CHIPS - 1)
    def _(s):
        dy, dz = offsets(s)
        pltpu.make_async_remote_copy(
            src_ref=tc.at[k, CHIPS - 1], dst_ref=tc.at[k, s], send_sem=ag_send,
            recv_sem=ag_recv.at[s // PER], device_id=chip(-dy, -dz), device_id_type=MESH).start()

    for c in loads:
        c.wait()

    def local_wait(ref, sem):
        pltpu.make_async_copy(ref, ref, sem).wait()

    def forward(c):
        block = tc.at[k, pl.ds(c * PER, PER)]
        return pltpu.make_async_remote_copy(
            src_ref=block, dst_ref=block, send_sem=fw_send.at[c], recv_sem=fw_recv.at[c],
            device_id=partner, device_id_type=MESH)

    def exchange(c):
        return pltpu.make_async_remote_copy(
            src_ref=part.at[c, 1 - k], dst_ref=pex.at[c], send_sem=pe_send.at[c],
            recv_sem=pe_recv.at[c], device_id=partner, device_id_type=MESH)

    def gather_stage(c):
        @pl.when(c < CHUNKS - 1)
        def _():
            local_wait(tc.at[k, pl.ds(c * PER, PER)], ag_recv.at[c])

        @pl.when(c == CHUNKS - 1)
        def _():
            local_wait(tc.at[k, pl.ds(c * PER, PER - 1)], ag_recv.at[c])

        forward(c).start()

    def first_stage(c):
        other = tc.at[1 - k, pl.ds(c * PER, PER)]
        local_wait(other, fw_recv.at[c])

        @pl.loop(0, 3)
        def _(g):
            rows = tc[g // 2, pl.ds(c * PER, PER)].reshape(CT, w.shape[2])
            p = lax.dot_general(w[g], rows, (((1,), (1,)), ((), ())), preferred_element_type=F32)
            p = p.reshape(NX, fx_rows, CT)
            pf[c, g] = p
            ps[c, :, g] = p.astype(BF)

        @pl.loop(1, NX)
        def _(r):
            pltpu.make_async_remote_copy(
                src_ref=ps.at[c, (x + r) % NX], dst_ref=pr.at[c, r - 1], send_sem=xr_send.at[c],
                recv_sem=xr_recv.at[c], device_id=xpeer(r), device_id_type=MESH).start()

    def point_stage(c):
        local_wait(pr.at[c], xr_recv.at[c])

        def total(g):
            return (pf[c, g, x] + pr[c, 0, g].astype(F32)
                    + pr[c, 1, g].astype(F32) + pr[c, 2, g].astype(F32))

        gate = total(0)
        up = total(1)
        slope = total(2)
        sig = 1.0 / (1.0 + jnp.exp(-gate))
        act = gate * sig
        hid[c, x, 0] = (slope * up * sig * (1.0 + gate * (1.0 - sig))).astype(BF)
        hid[c, x, 1] = (slope * act).astype(BF)
        hid[c, x, 2] = (act * up).astype(BF)

        @pl.loop(1, NX)
        def _(r):
            pltpu.make_async_remote_copy(
                src_ref=hid.at[c, x], dst_ref=hid.at[c, x], send_sem=xa_send.at[c],
                recv_sem=xa_recv.at[c], device_id=xpeer(r), device_id_type=MESH).start()

    def second_stage(c):
        local_wait(hid.at[c, pl.ds(0, NX - 1)], xa_recv.at[c])

        def prod(g):
            return lax.dot_general(hid[c, :, g].reshape(fpad, CT), w[g], (((0,), (0,)), ((), ())),
                                   preferred_element_type=F32)

        part[c, 0] = prod(2)
        part[c, 1] = prod(0) + prod(1)
        exchange(c).start()

    def scatter_stage(c):
        exchange(c).wait_recv()
        both = part[c, k] + pex[c]
        rs[pl.ds(c * PER, PER)] = both.astype(BF).reshape(PER, ROWS, both.shape[1])

        @pl.loop(c * PER, c * PER + PER - jnp.where(c == CHUNKS - 1, 1, 0))
        def _(s):
            dy, dz = offsets(s)
            pltpu.make_async_remote_copy(
                src_ref=rs.at[s], dst_ref=rr.at[s], send_sem=rs_send,
                recv_sem=rs_recv.at[c], device_id=chip(dy, dz), device_id_type=MESH).start()

    @pl.loop(0, CHUNKS + 3)
    def _(t):
        @pl.when(t < CHUNKS)
        def _():
            gather_stage(t)

        @pl.when(t >= 3)
        def _():
            scatter_stage(t - 3)

        @pl.when(t < CHUNKS)
        def _():
            first_stage(t)

        @pl.when((t >= 1) & (t < CHUNKS + 1))
        def _():
            point_stage(t - 1)

        @pl.when((t >= 2) & (t < CHUNKS + 2))
        def _():
            second_stage(t - 2)

    @pl.loop(0, 3)
    def _(g):
        h = jnp.concatenate([hid[c, :, g].reshape(fpad, CT) for c in range(CHUNKS)], axis=1)
        rows = tc[g // 2].reshape(CHUNKS * CT, w.shape[2])
        wout[g] = jnp.dot(h, rows, preferred_element_type=F32).astype(BF)

    stores = [
        pltpu.make_async_copy(wout.at[0, pl.ds(0, ff)], dgu_hbm.at[0], o_sem.at[0]),
        pltpu.make_async_copy(wout.at[1, pl.ds(0, ff)], dgu_hbm.at[1], o_sem.at[1]),
        pltpu.make_async_copy(wout.at[2, pl.ds(0, ff)], dd_hbm, o_sem.at[2]),
    ]
    for c in stores:
        c.start()

    acc[...] = rs[CHIPS - 1].astype(F32)
    for c in range(CHUNKS):
        n = PER if c < CHUNKS - 1 else PER - 1
        local_wait(rr.at[pl.ds(c * PER, n)], rs_recv.at[c])
        acc[...] += jnp.sum(rr[c * PER:c * PER + n].astype(F32), axis=0)

    low = acc[0:8, :]
    high = acc[8:16, :]
    fx[0] = jnp.where(first, high, low)
    back = pltpu.make_async_remote_copy(
        src_ref=fx.at[0], dst_ref=fx.at[1], send_sem=fx_sem.at[0], recv_sem=fx_sem.at[1],
        device_id=partner, device_id_type=MESH)
    back.start()

    local_wait(tc.at[0, pl.ds(0, CHIPS - 1)], ag_send)
    local_wait(rs.at[pl.ds(0, CHIPS - 1)], rs_send)

    @pl.loop(0, CHUNKS)
    def _(c):
        forward(c).wait_send()
        local_wait(pr.at[c], xr_send.at[c])
        local_wait(pr.at[c], xa_send.at[c])
        exchange(c).wait_send()

    back.wait()
    out_ref[...] = jnp.where(first, low, fx[1]).astype(BF)
    dtok_ref[...] = jnp.where(first, fx[1], high).astype(BF)
    for c in stores:
        c.wait()


def local(tokens, w_gate_up, w_down, cotangent):
    rows, d = tokens.shape
    ff = w_down.shape[0]
    fpad = -(-ff // (NX * ROWS)) * NX * ROWS
    fq = fpad // NX
    vm = pl.BlockSpec(memory_space=pltpu.VMEM)
    hbm = pl.BlockSpec(memory_space=pl.ANY)
    dma = pltpu.SemaphoreType.DMA
    out, d_tok, d_gu, d_down = pl.pallas_call(
        kernel,
        out_shape=(
            jax.ShapeDtypeStruct((rows, d), BF),
            jax.ShapeDtypeStruct((rows, d), BF),
            jax.ShapeDtypeStruct((2, ff, d), BF),
            jax.ShapeDtypeStruct((ff, d), BF),
        ),
        in_specs=[vm, vm, hbm, hbm],
        out_specs=(vm, vm, hbm, hbm),
        scratch_shapes=[
            pltpu.VMEM((3, fpad, d), BF),
            pltpu.VMEM((3, fpad, d), BF),
            pltpu.VMEM((2, CHIPS, ROWS, d), BF),
            pltpu.VMEM((2, rows, d), F32),
            pltpu.VMEM((CHUNKS, NX, 3, fq, CT), BF),
            pltpu.VMEM((CHUNKS, NX - 1, 3, fq, CT), BF),
            pltpu.VMEM((CHUNKS, 3, NX, fq, CT), F32),
            pltpu.VMEM((CHUNKS, NX, 3, fq, CT), BF),
            pltpu.VMEM((CHUNKS, 2, CT, d), F32),
            pltpu.VMEM((CHUNKS, CT, d), F32),
            pltpu.VMEM((CHIPS, ROWS, d), BF),
            pltpu.VMEM((CHIPS, ROWS, d), BF),
            pltpu.VMEM((ROWS, d), F32),
            pltpu.VMEM((2, rows, d), F32),
            dma((3,)), dma((3,)), dma((2,)),
            dma, dma((CHUNKS,)), dma((CHUNKS,)), dma((CHUNKS,)),
            dma((CHUNKS,)), dma((CHUNKS,)), dma((CHUNKS,)), dma((CHUNKS,)),
            dma((CHUNKS,)), dma((CHUNKS,)),
            dma, dma((CHUNKS,)), dma((2,)),
        ],
        compiler_params=pltpu.CompilerParams(
            collective_id=0, has_side_effects=True, vmem_limit_bytes=56 * 2**20),
    )(tokens, cotangent, w_gate_up, w_down)
    return out, d_tok, d_gu, d_down


def solution(mesh):
    placed = (
        P(("col", "dp"), "row"),
        P(None, ("col", "dp"), "row"),
        P(("col", "dp"), "row"),
        P(("col", "dp"), "row"),
    )
    return jax.shard_map(
        local,
        mesh=mesh,
        in_specs=placed,
        out_specs=(
            P(("col", "dp"), "row"),
            P(("col", "dp"), "row"),
            P(None, ("col", "dp"), "row"),
            P(("col", "dp"), "row"),
        ),
        check_vma=False,
    )
```

```python
import jax
import jax.numpy as jnp
from jax import lax
from jax.experimental import pallas as pl
from jax.experimental.pallas import tpu as pltpu
from jax.sharding import PartitionSpec as P

NX, NY, NZ = 4, 4, 8
CHIPS = NY * NZ
CHUNKS = 4
PER = CHIPS // CHUNKS
ROWS = 16
CT = PER * ROWS
HALF = CT // 2
Z_ORDER = (0, 1, 7, 2, 6, 3, 5, 4)
ZTABLE = sum(d << (3 * i) for i, d in enumerate(Z_ORDER))
ORDER = tuple((int(p[0]), int(p[1])) for p in (
    "00 01 10 20 02 11 21 30 03 12 22 31 40 50 13 23 32 41 60 51 33 42 61 52 43 62 53 63").split())
WORD = 10


def lookup(field, i):
    words = [sum(e[field] << (3 * j) for j, e in enumerate(ORDER[at:at + WORD]))
             for at in range(0, len(ORDER), WORD)]
    word = jnp.int32(words[0])
    for n, value in enumerate(words[1:], 1):
        word = jnp.where(i >= n * WORD, jnp.int32(value), word)
    return lax.shift_right_logical(word, 3 * (i % WORD)) % 8


BF = jnp.bfloat16
F32 = jnp.float32
MESH = pl.DeviceIdType.MESH


def kernel(tok_ref, cot_ref, wgu_hbm, wd_hbm, out_ref, dtok_ref, dgu_hbm, dd_hbm,
           w, wout, tc, rows, ps, pr, pf, hid, part, pex, rs, yk, yr, zs, zr, acc,
           w_sem, o_sem, az_send, az_recv, ay_send, ay_recv, fw_send, fw_recv,
           xr_send, xr_recv, xa_send, xa_recv, pe_send, pe_recv,
           sy_send, sy_recv, sz_send, sz_recv):
    x = lax.axis_index("row")
    col = lax.axis_index("col")
    dp = lax.axis_index("dp")
    k = col % 2
    y = dp % 4
    z = (dp // 4) * 2 + col // 2
    ff = wd_hbm.shape[0]
    fpad = w.shape[1]
    fx_rows = fpad // NX

    def chip(dy, dz):
        yy = (y + dy) % NY
        zz = (z + dz) % NZ
        return (x, (zz % 2) * 2 + k, (zz // 2) * 4 + yy)

    def zoff(p):
        return lax.shift_right_logical(jnp.int32(ZTABLE), 3 * p) % 8

    partner = (x, col + 1 - 2 * k, dp)

    def xpeer(r):
        return ((x + r) % NX, col, dp)

    loads = [
        pltpu.make_async_copy(wgu_hbm.at[0], w.at[0, pl.ds(0, ff)], w_sem.at[0]),
        pltpu.make_async_copy(wgu_hbm.at[1], w.at[1, pl.ds(0, ff)], w_sem.at[1]),
        pltpu.make_async_copy(wd_hbm, w.at[2, pl.ds(0, ff)], w_sem.at[2]),
    ]
    for c in loads:
        c.start()

    bar = pltpu.get_barrier_semaphore()
    pl.semaphore_signal(bar, inc=1, device_id=partner, device_id_type=MESH)

    @pl.loop(1, NZ)
    def _(d):
        pl.semaphore_signal(bar, inc=1, device_id=chip(0, d), device_id_type=MESH)

    @pl.loop(1, NY)
    def _(d):
        pl.semaphore_signal(bar, inc=1, device_id=chip(d, 0), device_id_type=MESH)

    @pl.loop(1, NX)
    def _(r):
        pl.semaphore_signal(bar, inc=1, device_id=xpeer(r), device_id_type=MESH)

    tc[0, k, 0] = jnp.concatenate(
        [tok_ref[...].astype(F32), cot_ref[...].astype(F32)], axis=0).astype(BF)
    if fpad > ff:
        w[:, pl.ds(ff, fpad - ff), :] = jnp.zeros((3, fpad - ff, w.shape[2]), BF)
    pl.semaphore_wait(bar, 1 + (NZ - 1) + (NY - 1) + (NX - 1))

    @pl.loop(1, NZ)
    def _(p):
        pltpu.make_async_remote_copy(
            src_ref=tc.at[0, k, 0], dst_ref=tc.at[p // 2, k, p % 2], send_sem=az_send,
            recv_sem=az_recv.at[p // 2], device_id=chip(0, -zoff(p)), device_id_type=MESH).start()

    for c in loads:
        c.wait()

    def local_wait(ref, sem):
        pltpu.make_async_copy(ref, ref, sem).wait()

    def forward(c):
        block = tc.at[c, k]
        return pltpu.make_async_remote_copy(
            src_ref=block, dst_ref=block, send_sem=fw_send.at[c], recv_sem=fw_recv.at[c],
            device_id=partner, device_id_type=MESH)

    def exchange(c):
        return pltpu.make_async_remote_copy(
            src_ref=part.at[c, :, pl.ds(pl.multiple_of((1 - k) * HALF, HALF), HALF)], dst_ref=pex.at[c], send_sem=pe_send.at[c],
            recv_sem=pe_recv.at[c], device_id=partner, device_id_type=MESH)

    def spread_stage(c):
        @pl.when(c == 0)
        def _():
            local_wait(tc.at[0, k, 0], az_recv.at[c])

        @pl.when(c > 0)
        def _():
            local_wait(tc.at[0, k, pl.ds(0, 2)], az_recv.at[c])

        @pl.loop(1, NY)
        def _(d):
            pltpu.make_async_remote_copy(
                src_ref=tc.at[c, k, pl.ds(0, 2)], dst_ref=tc.at[c, k, pl.ds(2 * d, 2)],
                send_sem=ay_send.at[c], recv_sem=ay_recv.at[c], device_id=chip(-d, 0),
                device_id_type=MESH).start()

    def gather_stage(c):
        local_wait(tc.at[c, k, pl.ds(2, PER - 2)], ay_recv.at[c])
        forward(c).start()

    def first_stage(c):
        local_wait(tc.at[c, 1 - k], fw_recv.at[c])

        @pl.loop(0, PER)
        def _(i):
            two = tc[c, i // (PER // 2), pl.ds((i % (PER // 2)) * 2, 2)].astype(F32)
            at = pl.ds(pl.multiple_of(c * CT + i * ROWS, ROWS), ROWS)
            rows[0, at] = two[:, 0:8].reshape(ROWS, w.shape[2]).astype(BF)
            rows[1, at] = two[:, 8:16].reshape(ROWS, w.shape[2]).astype(BF)

        @pl.loop(0, 3)
        def _(g):
            right = rows[g // 2, pl.ds(pl.multiple_of(c * CT, CT), CT)]
            p = lax.dot_general(w[g], right, (((1,), (1,)), ((), ())), preferred_element_type=F32)
            p = p.reshape(NX, fx_rows, CT)
            pf[c, g] = p
            ps[c, :, g] = p.astype(BF)

        @pl.loop(1, NX)
        def _(r):
            pltpu.make_async_remote_copy(
                src_ref=ps.at[c, (x + r) % NX], dst_ref=pr.at[c, r - 1], send_sem=xr_send.at[c],
                recv_sem=xr_recv.at[c], device_id=xpeer(r), device_id_type=MESH).start()

    def point_stage(c):
        local_wait(pr.at[c], xr_recv.at[c])

        def total(g):
            return (pf[c, g, x] + pr[c, 0, g].astype(F32)
                    + pr[c, 1, g].astype(F32) + pr[c, 2, g].astype(F32))

        gate = total(0)
        up = total(1)
        slope = total(2)
        sig = 1.0 / (1.0 + jnp.exp(-gate))
        act = gate * sig
        hid[c, x, 0] = (slope * up * sig * (1.0 + gate * (1.0 - sig))).astype(BF)
        hid[c, x, 1] = (slope * act).astype(BF)
        hid[c, x, 2] = (act * up).astype(BF)

        @pl.loop(1, NX)
        def _(r):
            pltpu.make_async_remote_copy(
                src_ref=hid.at[c, x], dst_ref=hid.at[c, x], send_sem=xa_send.at[c],
                recv_sem=xa_recv.at[c], device_id=xpeer(r), device_id_type=MESH).start()

    def second_stage(c):
        local_wait(hid.at[c, pl.ds(0, NX - 1)], xa_recv.at[c])

        def prod(g):
            return lax.dot_general(hid[c, :, g].reshape(fpad, CT), w[g], (((0,), (0,)), ((), ())),
                                   preferred_element_type=F32)

        part[c, 0] = prod(2)
        part[c, 1] = prod(0) + prod(1)
        exchange(c).start()

    def scatter_stage(c):
        exchange(c).wait_recv()

        @pl.loop(0, PER)
        def _(i):
            mine = pl.ds(pl.multiple_of(k * HALF + i * 8, 8), 8)
            theirs = pl.ds(pl.multiple_of(i * 8, 8), 8)
            both = part[c, :, mine] + pex[c, :, theirs]
            both = both.reshape(ROWS, both.shape[2])
            rs[c * PER + i] = both.astype(BF)

            @pl.when(i < 2)
            def _():
                yk[c, i] = both

        @pl.loop(1, NY)
        def _(d):
            pltpu.make_async_remote_copy(
                src_ref=rs.at[pl.ds(c * PER + 2 * d, 2)], dst_ref=yr.at[c, d - 1],
                send_sem=sy_send.at[c], recv_sem=sy_recv.at[c], device_id=chip(d, 0),
                device_id_type=MESH).start()

    def settle_stage(c):
        local_wait(yr.at[c], sy_recv.at[c])
        two = yk[c] + jnp.sum(yr[c].astype(F32), axis=0)
        zs[pl.ds(2 * c, 2)] = two.astype(BF)

        @pl.when(c == 0)
        def _():
            acc[...] = two[0]

        @pl.loop(2 * c + jnp.where(c == 0, 1, 0), 2 * c + 2)
        def _(p):
            pltpu.make_async_remote_copy(
                src_ref=zs.at[p], dst_ref=zr.at[p], send_sem=sz_send, recv_sem=sz_recv.at[c],
                device_id=chip(0, zoff(p)), device_id_type=MESH).start()

    stages = (spread_stage, gather_stage, first_stage, point_stage, second_stage,
              scatter_stage, settle_stage)

    @pl.loop(0, len(ORDER))
    def _(i):
        stage = lookup(0, i)
        c = lookup(1, i)
        for n, run in enumerate(stages):
            pl.when(stage == n)(lambda run=run: run(c))

    @pl.loop(0, 3)
    def _(g):
        h = jnp.concatenate([hid[c, :, g].reshape(fpad, CT) for c in range(CHUNKS)], axis=1)
        wout[g] = jnp.dot(h, rows[g // 2], preferred_element_type=F32).astype(BF)

    stores = [
        pltpu.make_async_copy(wout.at[0, pl.ds(0, ff)], dgu_hbm.at[0], o_sem.at[0]),
        pltpu.make_async_copy(wout.at[1, pl.ds(0, ff)], dgu_hbm.at[1], o_sem.at[1]),
        pltpu.make_async_copy(wout.at[2, pl.ds(0, ff)], dd_hbm, o_sem.at[2]),
    ]
    for c in stores:
        c.start()

    local_wait(zr.at[1], sz_recv.at[0])
    acc[...] += zr[1].astype(F32)
    for c in range(1, CHUNKS):
        local_wait(zr.at[pl.ds(2 * c, 2)], sz_recv.at[c])
        acc[...] += zr[2 * c].astype(F32) + zr[2 * c + 1].astype(F32)

    out_ref[...] = acc[0:8].astype(BF)
    dtok_ref[...] = acc[8:16].astype(BF)

    local_wait(zr.at[pl.ds(0, NZ - 1)], az_send)
    local_wait(zr.at[pl.ds(0, NZ - 1)], sz_send)

    @pl.loop(0, CHUNKS)
    def _(c):
        local_wait(yr.at[c], ay_send.at[c])
        local_wait(yr.at[c], sy_send.at[c])
        forward(c).wait_send()
        local_wait(pr.at[c], xr_send.at[c])
        local_wait(pr.at[c], xa_send.at[c])
        exchange(c).wait_send()

    for c in stores:
        c.wait()


def deliver(*refs):
    n = (len(refs) - 2) // 3
    srcs, dsts, bufs = refs[:n], refs[n:2 * n], refs[2 * n:3 * n]
    in_sems, out_sems = refs[3 * n:]
    steps = []
    for a, b, v in zip(srcs, dsts, bufs):
        rows = a.shape[-2]
        cuts = [pl.ds(0, rows)] if rows < 432 else [pl.ds(0, 224), pl.ds(224, rows - 224)]
        for g in range(a.shape[0]) if len(a.shape) == 3 else (None,):
            for cut in cuts:
                at = (cut,) if g is None else (g, cut)
                i = len(steps)
                steps.append((pltpu.make_async_copy(a.at[at], v.at[at], in_sems.at[i]),
                              pltpu.make_async_copy(v.at[at], b.at[at], out_sems.at[i])))
    for load, _ in steps:
        load.start()
    for load, store in steps:
        load.wait()
        store.start()
    for _, store in steps:
        store.wait()


def local(tokens, w_gate_up, w_down, cotangent):
    rows, d = tokens.shape
    ff = w_down.shape[0]
    fpad = -(-ff // (NX * ROWS)) * NX * ROWS
    fq = fpad // NX
    vm = pl.BlockSpec(memory_space=pltpu.VMEM)
    hbm = pl.BlockSpec(memory_space=pl.ANY)
    dma = pltpu.SemaphoreType.DMA
    results = pl.pallas_call(
        kernel,
        out_shape=(
            jax.ShapeDtypeStruct((rows, d), BF),
            jax.ShapeDtypeStruct((rows, d), BF),
            jax.ShapeDtypeStruct((2, ff, d), BF),
            jax.ShapeDtypeStruct((ff, d), BF),
        ),
        in_specs=[vm, vm, hbm, hbm],
        out_specs=(vm, vm, hbm, hbm),
        scratch_shapes=[
            pltpu.VMEM((3, fpad, d), BF),
            pltpu.VMEM((3, fpad, d), BF),
            pltpu.VMEM((CHUNKS, 2, PER, ROWS, d), BF),
            pltpu.VMEM((2, CHUNKS * CT, d), BF),
            pltpu.VMEM((CHUNKS, NX, 3, fq, CT), BF),
            pltpu.VMEM((CHUNKS, NX - 1, 3, fq, CT), BF),
            pltpu.VMEM((CHUNKS, 3, NX, fq, CT), F32),
            pltpu.VMEM((CHUNKS, NX, 3, fq, CT), BF),
            pltpu.VMEM((CHUNKS, 2, CT, d), F32),
            pltpu.VMEM((CHUNKS, 2, HALF, d), F32),
            pltpu.VMEM((CHIPS, ROWS, d), BF),
            pltpu.VMEM((CHUNKS, 2, ROWS, d), F32),
            pltpu.VMEM((CHUNKS, NY - 1, 2, ROWS, d), BF),
            pltpu.VMEM((NZ, ROWS, d), BF),
            pltpu.VMEM((NZ, ROWS, d), BF),
            pltpu.VMEM((ROWS, d), F32),
            dma((3,)), dma((3,)),
            dma, dma((CHUNKS,)), dma((CHUNKS,)), dma((CHUNKS,)), dma((CHUNKS,)), dma((CHUNKS,)),
            dma((CHUNKS,)), dma((CHUNKS,)), dma((CHUNKS,)), dma((CHUNKS,)),
            dma((CHUNKS,)), dma((CHUNKS,)),
            dma((CHUNKS,)), dma((CHUNKS,)), dma, dma((CHUNKS,)),
        ],
        compiler_params=pltpu.CompilerParams(
            collective_id=0, has_side_effects=True, vmem_limit_bytes=56 * 2**20),
    )(tokens, cotangent, w_gate_up, w_down)
    return pl.pallas_call(
        deliver,
        out_shape=tuple(jax.ShapeDtypeStruct(r.shape, r.dtype) for r in results),
        in_specs=[hbm] * len(results),
        out_specs=(hbm,) * len(results),
        scratch_shapes=[pltpu.VMEM(r.shape, r.dtype) for r in results] + [dma((8,)), dma((8,))],
        compiler_params=pltpu.CompilerParams(vmem_limit_bytes=56 * 2**20),
    )(*results)


def solution(mesh):
    placed = (
        P(("col", "dp"), "row"),
        P(None, ("col", "dp"), "row"),
        P(("col", "dp"), "row"),
        P(("col", "dp"), "row"),
    )
    return jax.shard_map(
        local,
        mesh=mesh,
        in_specs=placed,
        out_specs=(
            P(("col", "dp"), "row"),
            P(("col", "dp"), "row"),
            P(None, ("col", "dp"), "row"),
            P(("col", "dp"), "row"),
        ),
        check_vma=False,
    )
```

```python
import jax
import jax.numpy as jnp
from jax import lax
from jax.experimental import pallas as pl
from jax.experimental.pallas import tpu as pltpu
from jax.sharding import PartitionSpec as P

NX, NY, NZ = 4, 4, 8
CHIPS = NY * NZ
CHUNKS = 4
PER = CHIPS // CHUNKS
ROWS = 16
CT = PER * ROWS
HALF = CT // 2
Z_ORDER = (7, 2, 6, 3, 5, 4, 0, 1)
LAST = CHUNKS - 1
ZTABLE = sum(d << (3 * i) for i, d in enumerate(Z_ORDER))
ORDER = (0, 1, 10, 20, 2, 11, 21, 30, 3, 12, 22, 31, 40, 50, 13, 23, 32, 41, 60, 51, 33, 42, 61,
         52, 43, 53, 62, 70, 71, 72)
EARLY, LATE = 4, 0
WORD = 10


def lookup(field, i):
    words = [sum((e // 10, e % 10)[field] << (3 * j) for j, e in enumerate(ORDER[at:at + WORD]))
             for at in range(0, len(ORDER), WORD)]
    word = jnp.int32(words[0])
    for n, value in enumerate(words[1:], 1):
        word = jnp.where(i >= n * WORD, jnp.int32(value), word)
    return lax.shift_right_logical(word, 3 * (i % WORD)) % 8


BF = jnp.bfloat16
F32 = jnp.float32
MESH = pl.DeviceIdType.MESH


def kernel(tok_ref, cot_ref, wgu_hbm, wd_hbm, out_ref, dtok_ref, dgu_hbm, dd_hbm,
           w, wout, tc, rows, ps, pr, pf, hid, part, pex, rs, yk, yr, zs, zr, lr, acc,
           w_sem, o_sem, az_send, az_recv, ay_send, ay_recv, fw_send, fw_recv,
           xr_send, xr_recv, xa_send, xa_recv, pe_send, pe_recv,
           sy_send, sy_recv, sz_send, sz_recv):
    x = lax.axis_index("row")
    col = lax.axis_index("col")
    dp = lax.axis_index("dp")
    k = col % 2
    y = dp % 4
    z = (dp // 4) * 2 + col // 2
    ff = wd_hbm.shape[0]
    fpad = w.shape[1]
    fx_rows = fpad // NX

    def chip(dy, dz):
        yy = (y + dy) % NY
        zz = (z + dz) % NZ
        return (x, (zz % 2) * 2 + k, (zz // 2) * 4 + yy)

    def near(i):
        return jnp.where(i == 2, 2, 2 * i + 1)

    def zoff(p):
        return lax.shift_right_logical(jnp.int32(ZTABLE), 3 * p) % 8

    partner = (x, col + 1 - 2 * k, dp)

    def xpeer(r):
        return ((x + r) % NX, col, dp)

    loads = [
        pltpu.make_async_copy(wgu_hbm.at[0], w.at[0, pl.ds(0, ff)], w_sem.at[0]),
        pltpu.make_async_copy(wgu_hbm.at[1], w.at[1, pl.ds(0, ff)], w_sem.at[1]),
        pltpu.make_async_copy(wd_hbm, w.at[2, pl.ds(0, ff)], w_sem.at[2]),
    ]
    for c in loads:
        c.start()

    bar = pltpu.get_barrier_semaphore()
    pl.semaphore_signal(bar, inc=1, device_id=partner, device_id_type=MESH)

    @pl.loop(1, NZ)
    def _(d):
        pl.semaphore_signal(bar, inc=1, device_id=chip(0, d), device_id_type=MESH)

    @pl.loop(0, (NY - 1) * 3)
    def _(i):
        pl.semaphore_signal(bar, inc=1, device_id=chip(1 + i // 3, i % 3 - 1), device_id_type=MESH)

    @pl.loop(1, NX)
    def _(r):
        pl.semaphore_signal(bar, inc=1, device_id=xpeer(r), device_id_type=MESH)

    tc[LAST, k, 0] = jnp.concatenate(
        [tok_ref[...].astype(F32), cot_ref[...].astype(F32)], axis=0).astype(BF)
    if fpad > ff:
        w[:, pl.ds(ff, fpad - ff), :] = jnp.zeros((3, fpad - ff, w.shape[2]), BF)
    pl.semaphore_wait(bar, 1 + (NZ - 1) + (NY - 1) * 3 + (NX - 1))

    mine = tc.at[LAST, k, 0]

    def along_z(start, stop):
        @pl.loop(start, stop)
        def _(i):
            p = i + jnp.where(i >= 2 * LAST, 1, 0)
            pltpu.make_async_remote_copy(
                src_ref=mine, dst_ref=tc.at[p // 2, k, p % 2], send_sem=az_send,
                recv_sem=az_recv.at[p // 2], device_id=chip(0, -zoff(p)),
                device_id_type=MESH).start()

    along_z(0, EARLY)

    for c in loads:
        c.wait()

    def local_wait(ref, sem):
        pltpu.make_async_copy(ref, ref, sem).wait()

    def forward(c):
        block = tc.at[c, k]
        return pltpu.make_async_remote_copy(
            src_ref=block, dst_ref=block, send_sem=fw_send.at[c], recv_sem=fw_recv.at[c],
            device_id=partner, device_id_type=MESH)

    def exchange(c):
        return pltpu.make_async_remote_copy(
            src_ref=part.at[c, :, pl.ds(pl.multiple_of((1 - k) * HALF, HALF), HALF)], dst_ref=pex.at[c], send_sem=pe_send.at[c],
            recv_sem=pe_recv.at[c], device_id=partner, device_id_type=MESH)

    def spread_stage(c):
        @pl.when(c == LAST)
        def _():
            local_wait(tc.at[c, k, 1], az_recv.at[c])

        @pl.when(c < LAST)
        def _():
            local_wait(tc.at[c, k, pl.ds(0, 2)], az_recv.at[c])

        @pl.loop(0, NY - 1)
        def _(i):
            d = near(i)
            pltpu.make_async_remote_copy(
                src_ref=tc.at[c, k, pl.ds(0, 2)], dst_ref=tc.at[c, k, pl.ds(2 * d, 2)],
                send_sem=ay_send.at[c], recv_sem=ay_recv.at[c], device_id=chip(-d, 0),
                device_id_type=MESH).start()

        @pl.when(c == LATE)
        def _():
            along_z(EARLY, NZ - 1)

    def gather_stage(c):
        local_wait(tc.at[c, k, pl.ds(2, PER - 2)], ay_recv.at[c])

        forward(c).start()

    def first_stage(c):
        local_wait(tc.at[c, 1 - k], fw_recv.at[c])

        @pl.loop(0, PER)
        def _(i):
            two = tc[c, i // (PER // 2), pl.ds((i % (PER // 2)) * 2, 2)].astype(F32)
            at = pl.ds(pl.multiple_of(c * CT + i * ROWS, ROWS), ROWS)
            rows[0, at] = two[:, 0:8].reshape(ROWS, w.shape[2]).astype(BF)
            rows[1, at] = two[:, 8:16].reshape(ROWS, w.shape[2]).astype(BF)

        @pl.loop(0, 3)
        def _(g):
            right = rows[g // 2, pl.ds(pl.multiple_of(c * CT, CT), CT)]
            p = lax.dot_general(w[g], right, (((1,), (1,)), ((), ())), preferred_element_type=F32)
            p = p.reshape(NX, fx_rows, CT)
            pf[c, g] = p
            ps[c, :, g] = p.astype(BF)

        @pl.loop(0, NX - 1)
        def _(i):
            r = near(i)
            pltpu.make_async_remote_copy(
                src_ref=ps.at[c, (x + r) % NX], dst_ref=pr.at[c, r - 1], send_sem=xr_send.at[c],
                recv_sem=xr_recv.at[c], device_id=xpeer(r), device_id_type=MESH).start()

    def point_stage(c):
        local_wait(pr.at[c], xr_recv.at[c])

        def total(g):
            return (pf[c, g, x] + pr[c, 0, g].astype(F32)
                    + pr[c, 1, g].astype(F32) + pr[c, 2, g].astype(F32))

        gate = total(0)
        up = total(1)
        slope = total(2)
        sig = 1.0 / (1.0 + jnp.exp(-gate))
        act = gate * sig
        hid[c, x, 0] = (slope * up * sig * (1.0 + gate * (1.0 - sig))).astype(BF)
        hid[c, x, 1] = (slope * act).astype(BF)
        hid[c, x, 2] = (act * up).astype(BF)

        @pl.loop(0, NX - 1)
        def _(i):
            r = near(i)
            pltpu.make_async_remote_copy(
                src_ref=hid.at[c, x], dst_ref=hid.at[c, x], send_sem=xa_send.at[c],
                recv_sem=xa_recv.at[c], device_id=xpeer(r), device_id_type=MESH).start()

    def second_stage(c):
        local_wait(hid.at[c, pl.ds(0, NX - 1)], xa_recv.at[c])

        def prod(g):
            return lax.dot_general(hid[c, :, g].reshape(fpad, CT), w[g], (((0,), (0,)), ((), ())),
                                   preferred_element_type=F32)

        part[c, 0] = prod(2)
        part[c, 1] = prod(0) + prod(1)
        exchange(c).start()

    def scatter_stage(c):
        exchange(c).wait_recv()

        @pl.loop(0, PER)
        def _(i):
            mine = pl.ds(pl.multiple_of(k * HALF + i * 8, 8), 8)
            theirs = pl.ds(pl.multiple_of(i * 8, 8), 8)
            both = part[c, :, mine] + pex[c, :, theirs]
            both = both.reshape(ROWS, both.shape[2])
            rs[c * PER + i] = both.astype(BF)

            @pl.when(i < 2)
            def _():
                yk[c, i] = both

        @pl.when(c < LAST)
        def _():
            @pl.loop(0, NY - 1)
            def _(i):
                d = near(i)
                pltpu.make_async_remote_copy(
                    src_ref=rs.at[pl.ds(c * PER + 2 * d, 2)], dst_ref=yr.at[c, d - 1],
                    send_sem=sy_send.at[c], recv_sem=sy_recv.at[c], device_id=chip(d, 0),
                    device_id_type=MESH).start()

        @pl.when(c == LAST)
        def _():
            @pl.loop(1, PER)
            def _(i):
                pltpu.make_async_remote_copy(
                    src_ref=rs.at[LAST * PER + i], dst_ref=lr.at[i - 1], send_sem=sy_send.at[LAST],
                    recv_sem=sy_recv.at[LAST], device_id=chip(i // 2, zoff(2 * LAST + i % 2)),
                    device_id_type=MESH).start()

    def settle_stage(c):
        local_wait(yr.at[c], sy_recv.at[c])
        two = yk[c] + jnp.sum(yr[c].astype(F32), axis=0)
        zs[pl.ds(2 * c, 2)] = two.astype(BF)

        @pl.loop(2 * c, 2 * c + 2)
        def _(p):
            pltpu.make_async_remote_copy(
                src_ref=zs.at[p], dst_ref=zr.at[p], send_sem=sz_send, recv_sem=sz_recv.at[c],
                device_id=chip(0, zoff(p)), device_id_type=MESH).start()

    def weight_stage(g):
        h = jnp.concatenate([hid[c, :, g].reshape(fpad, CT) for c in range(CHUNKS)], axis=1)
        wout[g] = jnp.dot(h, rows[g // 2], preferred_element_type=F32).astype(BF)

    stages = (spread_stage, gather_stage, first_stage, point_stage, second_stage,
              scatter_stage, settle_stage, weight_stage)

    @pl.loop(0, len(ORDER))
    def _(i):
        stage = lookup(0, i)
        c = lookup(1, i)
        for n, run in enumerate(stages):
            pl.when(stage == n)(lambda run=run: run(c))

    stores = [
        pltpu.make_async_copy(wout.at[0, pl.ds(0, ff)], dgu_hbm.at[0], o_sem.at[0]),
        pltpu.make_async_copy(wout.at[1, pl.ds(0, ff)], dgu_hbm.at[1], o_sem.at[1]),
        pltpu.make_async_copy(wout.at[2, pl.ds(0, ff)], dd_hbm, o_sem.at[2]),
    ]
    for c in stores:
        c.start()

    acc[...] = yk[LAST, 0]
    for c in range(LAST):
        local_wait(zr.at[pl.ds(2 * c, 2)], sz_recv.at[c])
        acc[...] += zr[2 * c].astype(F32) + zr[2 * c + 1].astype(F32)
    local_wait(lr, sy_recv.at[LAST])
    acc[...] += jnp.sum(lr[...].astype(F32), axis=0)

    out_ref[...] = acc[0:8].astype(BF)
    dtok_ref[...] = acc[8:16].astype(BF)

    local_wait(lr, az_send)
    local_wait(zr, sz_send)
    local_wait(lr, sy_send.at[LAST])

    @pl.loop(0, CHUNKS)
    def _(c):
        local_wait(yr.at[0], ay_send.at[c])

        @pl.when(c < LAST)
        def _():
            local_wait(yr.at[0], sy_send.at[c])

        forward(c).wait_send()
        local_wait(pr.at[c], xr_send.at[c])
        local_wait(pr.at[c], xa_send.at[c])
        exchange(c).wait_send()

    for c in stores:
        c.wait()


def deliver(*refs):
    n = (len(refs) - 2) // 3
    srcs, dsts, bufs = refs[:n], refs[n:2 * n], refs[2 * n:3 * n]
    in_sems, out_sems = refs[3 * n:]
    steps = []
    for a, b, v in zip(srcs, dsts, bufs):
        rows = a.shape[-2]
        cuts = [pl.ds(0, rows)] if rows < 432 else [pl.ds(0, 224), pl.ds(224, rows - 224)]
        for g in range(a.shape[0]) if len(a.shape) == 3 else (None,):
            for cut in cuts:
                at = (cut,) if g is None else (g, cut)
                i = len(steps)
                steps.append((pltpu.make_async_copy(a.at[at], v.at[at], in_sems.at[i]),
                              pltpu.make_async_copy(v.at[at], b.at[at], out_sems.at[i])))
    for load, _ in steps:
        load.start()
    for load, store in steps:
        load.wait()
        store.start()
    for _, store in steps:
        store.wait()


def local(tokens, w_gate_up, w_down, cotangent):
    rows, d = tokens.shape
    ff = w_down.shape[0]
    fpad = -(-ff // (NX * ROWS)) * NX * ROWS
    fq = fpad // NX
    vm = pl.BlockSpec(memory_space=pltpu.VMEM)
    hbm = pl.BlockSpec(memory_space=pl.ANY)
    dma = pltpu.SemaphoreType.DMA
    results = pl.pallas_call(
        kernel,
        out_shape=(
            jax.ShapeDtypeStruct((rows, d), BF),
            jax.ShapeDtypeStruct((rows, d), BF),
            jax.ShapeDtypeStruct((2, ff, d), BF),
            jax.ShapeDtypeStruct((ff, d), BF),
        ),
        in_specs=[vm, vm, hbm, hbm],
        out_specs=(vm, vm, hbm, hbm),
        scratch_shapes=[
            pltpu.VMEM((3, fpad, d), BF),
            pltpu.VMEM((3, fpad, d), BF),
            pltpu.VMEM((CHUNKS, 2, PER, ROWS, d), BF),
            pltpu.VMEM((2, CHUNKS * CT, d), BF),
            pltpu.VMEM((CHUNKS, NX, 3, fq, CT), BF),
            pltpu.VMEM((CHUNKS, NX - 1, 3, fq, CT), BF),
            pltpu.VMEM((CHUNKS, 3, NX, fq, CT), F32),
            pltpu.VMEM((CHUNKS, NX, 3, fq, CT), BF),
            pltpu.VMEM((CHUNKS, 2, CT, d), F32),
            pltpu.VMEM((CHUNKS, 2, HALF, d), F32),
            pltpu.VMEM((CHIPS, ROWS, d), BF),
            pltpu.VMEM((CHUNKS, 2, ROWS, d), F32),
            pltpu.VMEM((CHUNKS - 1, NY - 1, 2, ROWS, d), BF),
            pltpu.VMEM((NZ - 2, ROWS, d), BF),
            pltpu.VMEM((NZ - 2, ROWS, d), BF),
            pltpu.VMEM((PER - 1, ROWS, d), BF),
            pltpu.VMEM((ROWS, d), F32),
            dma((3,)), dma((3,)),
            dma, dma((CHUNKS,)), dma((CHUNKS,)), dma((CHUNKS,)), dma((CHUNKS,)), dma((CHUNKS,)),
            dma((CHUNKS,)), dma((CHUNKS,)), dma((CHUNKS,)), dma((CHUNKS,)),
            dma((CHUNKS,)), dma((CHUNKS,)),
            dma((CHUNKS,)), dma((CHUNKS,)), dma, dma((CHUNKS,)),
        ],
        compiler_params=pltpu.CompilerParams(
            collective_id=0, has_side_effects=True, vmem_limit_bytes=56 * 2**20),
    )(tokens, cotangent, w_gate_up, w_down)
    return pl.pallas_call(
        deliver,
        out_shape=tuple(jax.ShapeDtypeStruct(r.shape, r.dtype) for r in results),
        in_specs=[hbm] * len(results),
        out_specs=(hbm,) * len(results),
        scratch_shapes=[pltpu.VMEM(r.shape, r.dtype) for r in results] + [dma((8,)), dma((8,))],
        compiler_params=pltpu.CompilerParams(vmem_limit_bytes=56 * 2**20),
    )(*results)


def solution(mesh):
    placed = (
        P(("col", "dp"), "row"),
        P(None, ("col", "dp"), "row"),
        P(("col", "dp"), "row"),
        P(("col", "dp"), "row"),
    )
    return jax.shard_map(
        local,
        mesh=mesh,
        in_specs=placed,
        out_specs=(
            P(("col", "dp"), "row"),
            P(("col", "dp"), "row"),
            P(None, ("col", "dp"), "row"),
            P(("col", "dp"), "row"),
        ),
        check_vma=False,
    )
```

```python
import jax
import jax.numpy as jnp
from jax import lax
from jax.experimental import pallas as pl
from jax.experimental.pallas import tpu as pltpu
from jax.sharding import PartitionSpec as P

NX, NY, NZ = 4, 4, 8
CHIPS = NY * NZ
CHUNKS = 4
PER = CHIPS // CHUNKS
ROWS = 16
CT = PER * ROWS
HALF = CT // 2
Z_ORDER = (7, 2, 6, 3, 5, 4, 0, 1)
LAST = CHUNKS - 1
ZTABLE = sum(d << (3 * i) for i, d in enumerate(Z_ORDER))
ORDER = (0, 1, 10, 20, 2, 11, 21, 12, 30, 3, 22, 31, 40, 50, 13, 23, 32, 41, 60, 51, 33, 42, 61,
         52, 43, 70, 71, 53, 62, 72)
EARLY, LATE = 4, 0
WORD = 10


def lookup(field, i):
    words = [sum((e // 10, e % 10)[field] << (3 * j) for j, e in enumerate(ORDER[at:at + WORD]))
             for at in range(0, len(ORDER), WORD)]
    word = jnp.int32(words[0])
    for n, value in enumerate(words[1:], 1):
        word = jnp.where(i >= n * WORD, jnp.int32(value), word)
    return lax.shift_right_logical(word, 3 * (i % WORD)) % 8


BF = jnp.bfloat16
F32 = jnp.float32
MESH = pl.DeviceIdType.MESH


def kernel(tok_ref, cot_ref, wgu_hbm, wd_hbm, out_ref, dtok_ref, dgu_hbm, dd_hbm,
           w, wout, tc, rows, ps, pr, pf, hid, part, pex, rs, yk, yr, zs, zr, lr, acc,
           w_sem, o_sem, az_send, az_recv, ay_send, ay_recv, fw_send, fw_recv,
           xr_send, xr_recv, xa_send, xa_recv, pe_send, pe_recv,
           sy_send, sy_recv, sz_send, sz_recv):
    x = lax.axis_index("row")
    col = lax.axis_index("col")
    dp = lax.axis_index("dp")
    k = col % 2
    y = dp % 4
    z = (dp // 4) * 2 + col // 2
    ff = wd_hbm.shape[0]
    fpad = w.shape[1]
    fx_rows = fpad // NX

    def chip(dy, dz):
        yy = (y + dy) % NY
        zz = (z + dz) % NZ
        return (x, (zz % 2) * 2 + k, (zz // 2) * 4 + yy)

    def near(i):
        return jnp.where(i == 2, 2, 2 * i + 1)

    def zoff(p):
        return lax.shift_right_logical(jnp.int32(ZTABLE), 3 * p) % 8

    partner = (x, col + 1 - 2 * k, dp)

    def xpeer(r):
        return ((x + r) % NX, col, dp)

    loads = [
        pltpu.make_async_copy(wgu_hbm.at[0], w.at[0, pl.ds(0, ff)], w_sem.at[0]),
        pltpu.make_async_copy(wgu_hbm.at[1], w.at[1, pl.ds(0, ff)], w_sem.at[1]),
        pltpu.make_async_copy(wd_hbm, w.at[2, pl.ds(0, ff)], w_sem.at[2]),
    ]
    for c in loads:
        c.start()

    bar = pltpu.get_barrier_semaphore()
    pl.semaphore_signal(bar, inc=1, device_id=partner, device_id_type=MESH)

    @pl.loop(1, NZ)
    def _(d):
        pl.semaphore_signal(bar, inc=1, device_id=chip(0, d), device_id_type=MESH)

    @pl.loop(0, (NY - 1) * 3)
    def _(i):
        pl.semaphore_signal(bar, inc=1, device_id=chip(1 + i // 3, i % 3 - 1), device_id_type=MESH)

    @pl.loop(1, NX)
    def _(r):
        pl.semaphore_signal(bar, inc=1, device_id=xpeer(r), device_id_type=MESH)

    tc[LAST, k, 0] = jnp.concatenate(
        [tok_ref[...].astype(F32), cot_ref[...].astype(F32)], axis=0).astype(BF)
    if fpad > ff:
        w[:, pl.ds(ff, fpad - ff), :] = jnp.zeros((3, fpad - ff, w.shape[2]), BF)
    pl.semaphore_wait(bar, 1 + (NZ - 1) + (NY - 1) * 3 + (NX - 1))

    mine = tc.at[LAST, k, 0]

    def along_z(start, stop):
        @pl.loop(start, stop)
        def _(i):
            p = i + jnp.where(i >= 2 * LAST, 1, 0)
            pltpu.make_async_remote_copy(
                src_ref=mine, dst_ref=tc.at[p // 2, k, p % 2], send_sem=az_send,
                recv_sem=az_recv.at[p // 2], device_id=chip(0, -zoff(p)),
                device_id_type=MESH).start()

    along_z(0, EARLY)

    for c in loads:
        c.wait()

    def local_wait(ref, sem):
        pltpu.make_async_copy(ref, ref, sem).wait()

    def forward(c):
        block = tc.at[c, k]
        return pltpu.make_async_remote_copy(
            src_ref=block, dst_ref=block, send_sem=fw_send.at[c], recv_sem=fw_recv.at[c],
            device_id=partner, device_id_type=MESH)

    def exchange(c):
        return pltpu.make_async_remote_copy(
            src_ref=part.at[c, :, pl.ds(pl.multiple_of((1 - k) * HALF, HALF), HALF)], dst_ref=pex.at[c], send_sem=pe_send.at[c],
            recv_sem=pe_recv.at[c], device_id=partner, device_id_type=MESH)

    def spread_stage(c):
        @pl.when(c == LAST)
        def _():
            local_wait(tc.at[c, k, 1], az_recv.at[c])

        @pl.when(c < LAST)
        def _():
            local_wait(tc.at[c, k, pl.ds(0, 2)], az_recv.at[c])

        @pl.loop(0, NY - 1)
        def _(i):
            d = near(i)
            pltpu.make_async_remote_copy(
                src_ref=tc.at[c, k, pl.ds(0, 2)], dst_ref=tc.at[c, k, pl.ds(2 * d, 2)],
                send_sem=ay_send.at[c], recv_sem=ay_recv.at[c], device_id=chip(-d, 0),
                device_id_type=MESH).start()

        @pl.when(c == LATE)
        def _():
            along_z(EARLY, NZ - 1)

    def lay_rows(c, core):
        @pl.loop(0, PER // 2)
        def _(i):
            two = tc[c, core, pl.ds(2 * i, 2)].astype(F32)
            at = pl.ds(pl.multiple_of(c * CT + core * HALF + i * ROWS, ROWS), ROWS)
            rows[0, at] = two[:, 0:8].reshape(ROWS, w.shape[2]).astype(BF)
            rows[1, at] = two[:, 8:16].reshape(ROWS, w.shape[2]).astype(BF)

    def gather_stage(c):
        local_wait(tc.at[c, k, pl.ds(2, PER - 2)], ay_recv.at[c])

        forward(c).start()
        lay_rows(c, k)

    def first_stage(c):
        local_wait(tc.at[c, 1 - k], fw_recv.at[c])

        lay_rows(c, 1 - k)

        @pl.loop(0, 3)
        def _(g):
            right = rows[g // 2, pl.ds(pl.multiple_of(c * CT, CT), CT)]
            p = lax.dot_general(w[g], right, (((1,), (1,)), ((), ())), preferred_element_type=F32)
            p = p.reshape(NX, fx_rows, CT)
            pf[c, g] = p
            ps[c, :, g] = p.astype(BF)

            @pl.loop(0, NX - 1)
            def _(i):
                r = near(i)
                pltpu.make_async_remote_copy(
                    src_ref=ps.at[c, (x + r) % NX, g], dst_ref=pr.at[c, r - 1, g],
                    send_sem=xr_send.at[c], recv_sem=xr_recv.at[c], device_id=xpeer(r),
                    device_id_type=MESH).start()

    def point_stage(c):
        local_wait(pr.at[c], xr_recv.at[c])

        def total(g):
            return (pf[c, g, x] + pr[c, 0, g].astype(F32)
                    + pr[c, 1, g].astype(F32) + pr[c, 2, g].astype(F32))

        gate = total(0)
        up = total(1)
        slope = total(2)
        sig = 1.0 / (1.0 + jnp.exp(-gate))
        act = gate * sig
        hid[c, x, 0] = (slope * up * sig * (1.0 + gate * (1.0 - sig))).astype(BF)
        hid[c, x, 1] = (slope * act).astype(BF)
        hid[c, x, 2] = (act * up).astype(BF)

        @pl.loop(0, NX - 1)
        def _(i):
            r = near(i)
            pltpu.make_async_remote_copy(
                src_ref=hid.at[c, x], dst_ref=hid.at[c, x], send_sem=xa_send.at[c],
                recv_sem=xa_recv.at[c], device_id=xpeer(r), device_id_type=MESH).start()

    def second_stage(c):
        local_wait(hid.at[c, pl.ds(0, NX - 1)], xa_recv.at[c])

        def prod(g):
            return lax.dot_general(hid[c, :, g].reshape(fpad, CT), w[g], (((0,), (0,)), ((), ())),
                                   preferred_element_type=F32)

        part[c, 0] = prod(2)
        part[c, 1] = prod(0) + prod(1)
        exchange(c).start()

    def scatter_stage(c):
        exchange(c).wait_recv()

        @pl.loop(0, PER)
        def _(i):
            mine = pl.ds(pl.multiple_of(k * HALF + i * 8, 8), 8)
            theirs = pl.ds(pl.multiple_of(i * 8, 8), 8)
            both = part[c, :, mine] + pex[c, :, theirs]
            both = both.reshape(ROWS, both.shape[2])
            rs[c * PER + i] = both.astype(BF)

            @pl.when(i < 2)
            def _():
                yk[c, i] = both

        @pl.when(c < LAST)
        def _():
            @pl.loop(0, NY - 1)
            def _(i):
                d = near(i)
                pltpu.make_async_remote_copy(
                    src_ref=rs.at[pl.ds(c * PER + 2 * d, 2)], dst_ref=yr.at[c, d - 1],
                    send_sem=sy_send.at[c], recv_sem=sy_recv.at[c], device_id=chip(d, 0),
                    device_id_type=MESH).start()

        @pl.when(c == LAST)
        def _():
            @pl.loop(1, PER)
            def _(i):
                pltpu.make_async_remote_copy(
                    src_ref=rs.at[LAST * PER + i], dst_ref=lr.at[i - 1], send_sem=sy_send.at[LAST],
                    recv_sem=sy_recv.at[LAST], device_id=chip(i // 2, zoff(2 * LAST + i % 2)),
                    device_id_type=MESH).start()

    def settle_stage(c):
        local_wait(yr.at[c], sy_recv.at[c])
        two = yk[c] + jnp.sum(yr[c].astype(F32), axis=0)
        zs[pl.ds(2 * c, 2)] = two.astype(BF)

        @pl.loop(2 * c, 2 * c + 2)
        def _(p):
            pltpu.make_async_remote_copy(
                src_ref=zs.at[p], dst_ref=zr.at[p], send_sem=sz_send, recv_sem=sz_recv.at[c],
                device_id=chip(0, zoff(p)), device_id_type=MESH).start()

    stores = [
        pltpu.make_async_copy(wout.at[0, pl.ds(0, ff)], dgu_hbm.at[0], o_sem.at[0]),
        pltpu.make_async_copy(wout.at[1, pl.ds(0, ff)], dgu_hbm.at[1], o_sem.at[1]),
        pltpu.make_async_copy(wout.at[2, pl.ds(0, ff)], dd_hbm, o_sem.at[2]),
    ]

    def weight_stage(g):
        h = jnp.concatenate([hid[c, :, g].reshape(fpad, CT) for c in range(CHUNKS)], axis=1)
        wout[g] = jnp.dot(h, rows[g // 2], preferred_element_type=F32).astype(BF)
        for n, store in enumerate(stores):
            pl.when(g == n)(store.start)

    stages = (spread_stage, gather_stage, first_stage, point_stage, second_stage,
              scatter_stage, settle_stage, weight_stage)

    @pl.loop(0, len(ORDER))
    def _(i):
        stage = lookup(0, i)
        c = lookup(1, i)
        for n, run in enumerate(stages):
            pl.when(stage == n)(lambda run=run: run(c))

    acc[...] = yk[LAST, 0]
    for c in range(LAST):
        local_wait(zr.at[pl.ds(2 * c, 2)], sz_recv.at[c])
        acc[...] += zr[2 * c].astype(F32) + zr[2 * c + 1].astype(F32)
    local_wait(lr, sy_recv.at[LAST])
    acc[...] += jnp.sum(lr[...].astype(F32), axis=0)

    out_ref[...] = acc[0:8].astype(BF)
    dtok_ref[...] = acc[8:16].astype(BF)

    local_wait(lr, az_send)
    local_wait(zr, sz_send)
    local_wait(lr, sy_send.at[LAST])

    @pl.loop(0, CHUNKS)
    def _(c):
        local_wait(yr.at[0], ay_send.at[c])

        @pl.when(c < LAST)
        def _():
            local_wait(yr.at[0], sy_send.at[c])

        forward(c).wait_send()
        local_wait(pr.at[c], xr_send.at[c])
        local_wait(pr.at[c], xa_send.at[c])
        exchange(c).wait_send()

    for c in stores:
        c.wait()


def deliver(*refs):
    n = (len(refs) - 2) // 3
    srcs, dsts, bufs = refs[:n], refs[n:2 * n], refs[2 * n:3 * n]
    in_sems, out_sems = refs[3 * n:]
    steps = []
    for a, b, v in zip(srcs, dsts, bufs):
        rows = a.shape[-2]
        cuts = [pl.ds(0, rows)] if rows < 432 else [pl.ds(0, 224), pl.ds(224, rows - 224)]
        for g in range(a.shape[0]) if len(a.shape) == 3 else (None,):
            for cut in cuts:
                at = (cut,) if g is None else (g, cut)
                i = len(steps)
                steps.append((pltpu.make_async_copy(a.at[at], v.at[at], in_sems.at[i]),
                              pltpu.make_async_copy(v.at[at], b.at[at], out_sems.at[i])))
    for load, _ in steps:
        load.start()
    for load, store in steps:
        load.wait()
        store.start()
    for _, store in steps:
        store.wait()


def local(tokens, w_gate_up, w_down, cotangent):
    rows, d = tokens.shape
    ff = w_down.shape[0]
    fpad = -(-ff // (NX * ROWS)) * NX * ROWS
    fq = fpad // NX
    vm = pl.BlockSpec(memory_space=pltpu.VMEM)
    hbm = pl.BlockSpec(memory_space=pl.ANY)
    dma = pltpu.SemaphoreType.DMA
    results = pl.pallas_call(
        kernel,
        out_shape=(
            jax.ShapeDtypeStruct((rows, d), BF),
            jax.ShapeDtypeStruct((rows, d), BF),
            jax.ShapeDtypeStruct((2, ff, d), BF),
            jax.ShapeDtypeStruct((ff, d), BF),
        ),
        in_specs=[vm, vm, hbm, hbm],
        out_specs=(vm, vm, hbm, hbm),
        scratch_shapes=[
            pltpu.VMEM((3, fpad, d), BF),
            pltpu.VMEM((3, fpad, d), BF),
            pltpu.VMEM((CHUNKS, 2, PER, ROWS, d), BF),
            pltpu.VMEM((2, CHUNKS * CT, d), BF),
            pltpu.VMEM((CHUNKS, NX, 3, fq, CT), BF),
            pltpu.VMEM((CHUNKS, NX - 1, 3, fq, CT), BF),
            pltpu.VMEM((CHUNKS, 3, NX, fq, CT), F32),
            pltpu.VMEM((CHUNKS, NX, 3, fq, CT), BF),
            pltpu.VMEM((CHUNKS, 2, CT, d), F32),
            pltpu.VMEM((CHUNKS, 2, HALF, d), F32),
            pltpu.VMEM((CHIPS, ROWS, d), BF),
            pltpu.VMEM((CHUNKS, 2, ROWS, d), F32),
            pltpu.VMEM((CHUNKS - 1, NY - 1, 2, ROWS, d), BF),
            pltpu.VMEM((NZ - 2, ROWS, d), BF),
            pltpu.VMEM((NZ - 2, ROWS, d), BF),
            pltpu.VMEM((PER - 1, ROWS, d), BF),
            pltpu.VMEM((ROWS, d), F32),
            dma((3,)), dma((3,)),
            dma, dma((CHUNKS,)), dma((CHUNKS,)), dma((CHUNKS,)), dma((CHUNKS,)), dma((CHUNKS,)),
            dma((CHUNKS,)), dma((CHUNKS,)), dma((CHUNKS,)), dma((CHUNKS,)),
            dma((CHUNKS,)), dma((CHUNKS,)),
            dma((CHUNKS,)), dma((CHUNKS,)), dma, dma((CHUNKS,)),
        ],
        compiler_params=pltpu.CompilerParams(
            collective_id=0, has_side_effects=True, vmem_limit_bytes=56 * 2**20),
    )(tokens, cotangent, w_gate_up, w_down)
    return pl.pallas_call(
        deliver,
        out_shape=tuple(jax.ShapeDtypeStruct(r.shape, r.dtype) for r in results),
        in_specs=[hbm] * len(results),
        out_specs=(hbm,) * len(results),
        scratch_shapes=[pltpu.VMEM(r.shape, r.dtype) for r in results] + [dma((8,)), dma((8,))],
        compiler_params=pltpu.CompilerParams(vmem_limit_bytes=56 * 2**20),
    )(*results)


def solution(mesh):
    placed = (
        P(("col", "dp"), "row"),
        P(None, ("col", "dp"), "row"),
        P(("col", "dp"), "row"),
        P(("col", "dp"), "row"),
    )
    return jax.shard_map(
        local,
        mesh=mesh,
        in_specs=placed,
        out_specs=(
            P(("col", "dp"), "row"),
            P(("col", "dp"), "row"),
            P(None, ("col", "dp"), "row"),
            P(("col", "dp"), "row"),
        ),
        check_vma=False,
    )
```

```python
import jax
import jax.numpy as jnp
from jax import lax
from jax.experimental import pallas as pl
from jax.experimental.pallas import tpu as pltpu
from jax.sharding import PartitionSpec as P

NX, NY, NZ = 4, 4, 8
CHIPS = NY * NZ
CHUNKS = 4
PER = CHIPS // CHUNKS
ROWS = 16
CT = PER * ROWS
HALF = CT // 2
Z_ORDER = (7, 2, 6, 3, 5, 4, 0, 1)
LAST = CHUNKS - 1
ZTABLE = sum(d << (3 * i) for i, d in enumerate(Z_ORDER))
ORDER = (0, 1, 10, 20, 2, 11, 21, 12, 30, 3, 22, 31, 40, 50, 13, 23, 32, 41, 60, 51, 33, 42, 61,
         52, 43, 70, 71, 53, 62, 72)
EARLY, LATE = 4, 0
WORD = 10


def lookup(field, i):
    words = [sum((e // 10, e % 10)[field] << (3 * j) for j, e in enumerate(ORDER[at:at + WORD]))
             for at in range(0, len(ORDER), WORD)]
    word = jnp.int32(words[0])
    for n, value in enumerate(words[1:], 1):
        word = jnp.where(i >= n * WORD, jnp.int32(value), word)
    return lax.shift_right_logical(word, 3 * (i % WORD)) % 8


BF = jnp.bfloat16
F32 = jnp.float32
MESH = pl.DeviceIdType.MESH


def kernel(tok_ref, cot_ref, wgu_hbm, wd_hbm, out_ref, dtok_ref, dgu_hbm, dd_hbm,
           w, wout, tc, rows, ps, pr, pf, hid, part, pex, rs, yk, yr, zs, zr, lr, acc,
           w_sem, o_sem, az_send, az_recv, ay_send, ay_recv, fw_send, fw_recv,
           xr_send, xr_recv, xa_send, xa_recv, pe_send, pe_recv,
           sy_send, sy_recv, sz_send, sz_recv):
    x = lax.axis_index("row")
    col = lax.axis_index("col")
    dp = lax.axis_index("dp")
    k = col % 2
    y = dp % 4
    z = (dp // 4) * 2 + col // 2
    ff = wd_hbm.shape[0]
    fpad = w.shape[1]
    fx_rows = fpad // NX

    def chip(dy, dz):
        yy = (y + dy) % NY
        zz = (z + dz) % NZ
        return (x, (zz % 2) * 2 + k, (zz // 2) * 4 + yy)

    def near(i):
        return jnp.where(i == 2, 2, 2 * i + 1)

    def zoff(p):
        return lax.shift_right_logical(jnp.int32(ZTABLE), 3 * p) % 8

    partner = (x, col + 1 - 2 * k, dp)

    def xpeer(r):
        return ((x + r) % NX, col, dp)

    loads = [
        pltpu.make_async_copy(wgu_hbm.at[0], w.at[0, pl.ds(0, ff)], w_sem.at[0]),
        pltpu.make_async_copy(wgu_hbm.at[1], w.at[1, pl.ds(0, ff)], w_sem.at[1]),
        pltpu.make_async_copy(wd_hbm, w.at[2, pl.ds(0, ff)], w_sem.at[2]),
    ]
    for c in loads:
        c.start()

    bar = pltpu.get_barrier_semaphore()
    pl.semaphore_signal(bar, inc=1, device_id=partner, device_id_type=MESH)

    @pl.loop(1, NZ)
    def _(d):
        pl.semaphore_signal(bar, inc=1, device_id=chip(0, d), device_id_type=MESH)

    @pl.loop(0, (NY - 1) * 3)
    def _(i):
        pl.semaphore_signal(bar, inc=1, device_id=chip(1 + i // 3, i % 3 - 1), device_id_type=MESH)

    @pl.loop(1, NX)
    def _(r):
        pl.semaphore_signal(bar, inc=1, device_id=xpeer(r), device_id_type=MESH)

    tc[LAST, k, 0] = jnp.concatenate(
        [tok_ref[...].astype(F32), cot_ref[...].astype(F32)], axis=0).astype(BF)
    if fpad > ff:
        w[:, pl.ds(ff, fpad - ff), :] = jnp.zeros((3, fpad - ff, w.shape[2]), BF)
    pl.semaphore_wait(bar, 1 + (NZ - 1) + (NY - 1) * 3 + (NX - 1))

    mine = tc.at[LAST, k, 0]

    def along_z(start, stop):
        @pl.loop(start, stop)
        def _(i):
            p = i + jnp.where(i >= 2 * LAST, 1, 0)
            pltpu.make_async_remote_copy(
                src_ref=mine, dst_ref=tc.at[p // 2, k, p % 2], send_sem=az_send,
                recv_sem=az_recv.at[p // 2], device_id=chip(0, -zoff(p)),
                device_id_type=MESH).start()

    along_z(0, EARLY)

    for c in loads:
        c.wait()

    def local_wait(ref, sem):
        pltpu.make_async_copy(ref, ref, sem).wait()

    def forward(c):
        block = tc.at[c, k]
        return pltpu.make_async_remote_copy(
            src_ref=block, dst_ref=block, send_sem=fw_send.at[c], recv_sem=fw_recv.at[c],
            device_id=partner, device_id_type=MESH)

    def exchange(c):
        return pltpu.make_async_remote_copy(
            src_ref=part.at[c, :, pl.ds(pl.multiple_of((1 - k) * HALF, HALF), HALF)], dst_ref=pex.at[c], send_sem=pe_send.at[c],
            recv_sem=pe_recv.at[c], device_id=partner, device_id_type=MESH)

    def spread_stage(c):
        @pl.when(c == LAST)
        def _():
            local_wait(tc.at[c, k, 1], az_recv.at[c])

        @pl.when(c < LAST)
        def _():
            local_wait(tc.at[c, k, pl.ds(0, 2)], az_recv.at[c])

        @pl.loop(0, NY - 1)
        def _(i):
            d = near(i)
            pltpu.make_async_remote_copy(
                src_ref=tc.at[c, k, pl.ds(0, 2)], dst_ref=tc.at[c, k, pl.ds(2 * d, 2)],
                send_sem=ay_send.at[c], recv_sem=ay_recv.at[c], device_id=chip(-d, 0),
                device_id_type=MESH).start()

        @pl.when(c == LATE)
        def _():
            along_z(EARLY, NZ - 1)

    def lay_rows(c, core):
        @pl.loop(0, PER // 2)
        def _(i):
            two = tc[c, core, pl.ds(2 * i, 2)].astype(F32)
            at = pl.ds(pl.multiple_of(c * CT + core * HALF + i * ROWS, ROWS), ROWS)
            rows[0, at] = two[:, 0:8].reshape(ROWS, w.shape[2]).astype(BF)
            rows[1, at] = two[:, 8:16].reshape(ROWS, w.shape[2]).astype(BF)

    def gather_stage(c):
        local_wait(tc.at[c, k, pl.ds(2, PER - 2)], ay_recv.at[c])

        forward(c).start()
        lay_rows(c, k)

    def first_stage(c):
        local_wait(tc.at[c, 1 - k], fw_recv.at[c])

        lay_rows(c, 1 - k)

        @pl.loop(0, 3)
        def _(g):
            right = rows[g // 2, pl.ds(pl.multiple_of(c * CT, CT), CT)]
            p = lax.dot_general(w[g], right, (((1,), (1,)), ((), ())), preferred_element_type=F32)
            p = p.reshape(NX, fx_rows, CT)
            pf[c, g] = p
            ps[c, :, g] = p.astype(BF)

            @pl.loop(0, NX - 1)
            def _(i):
                r = near(i)
                pltpu.make_async_remote_copy(
                    src_ref=ps.at[c, (x + r) % NX, g], dst_ref=pr.at[c, r - 1, g],
                    send_sem=xr_send.at[c], recv_sem=xr_recv.at[c], device_id=xpeer(r),
                    device_id_type=MESH).start()

    def share(c, which):
        block = hid.at[c, x, which]

        @pl.loop(0, NX - 1)
        def _(i):
            pltpu.make_async_remote_copy(
                src_ref=block, dst_ref=block, send_sem=xa_send.at[c], recv_sem=xa_recv.at[c],
                device_id=xpeer(near(i)), device_id_type=MESH).start()

    def point_stage(c):
        local_wait(pr.at[c], xr_recv.at[c])

        def total(g):
            return (pf[c, g, x] + pr[c, 0, g].astype(F32)
                    + pr[c, 1, g].astype(F32) + pr[c, 2, g].astype(F32))

        gate = total(0)
        up = total(1)
        slope = total(2)
        sig = 1.0 / (1.0 + jnp.exp(-gate))
        act = gate * sig
        hid[c, x, 2] = (act * up).astype(BF)
        share(c, pl.ds(2, 1))
        hid[c, x, 0] = (slope * up * sig * (1.0 + gate * (1.0 - sig))).astype(BF)
        hid[c, x, 1] = (slope * act).astype(BF)
        share(c, pl.ds(0, 2))

    def second_stage(c):
        local_wait(hid.at[c, pl.ds(0, NX - 1)], xa_recv.at[c])

        def prod(g):
            return lax.dot_general(hid[c, :, g].reshape(fpad, CT), w[g], (((0,), (0,)), ((), ())),
                                   preferred_element_type=F32)

        part[c, 0] = prod(2)
        part[c, 1] = prod(0) + prod(1)
        exchange(c).start()

    def scatter_stage(c):
        exchange(c).wait_recv()

        @pl.loop(0, PER)
        def _(i):
            mine = pl.ds(pl.multiple_of(k * HALF + i * 8, 8), 8)
            theirs = pl.ds(pl.multiple_of(i * 8, 8), 8)
            both = part[c, :, mine] + pex[c, :, theirs]
            both = both.reshape(ROWS, both.shape[2])
            rs[c * PER + i] = both.astype(BF)

            @pl.when(i < 2)
            def _():
                yk[c, i] = both

        @pl.when(c < LAST)
        def _():
            @pl.loop(0, NY - 1)
            def _(i):
                d = near(i)
                pltpu.make_async_remote_copy(
                    src_ref=rs.at[pl.ds(c * PER + 2 * d, 2)], dst_ref=yr.at[c, d - 1],
                    send_sem=sy_send.at[c], recv_sem=sy_recv.at[c], device_id=chip(d, 0),
                    device_id_type=MESH).start()

        @pl.when(c == LAST)
        def _():
            @pl.loop(1, PER)
            def _(i):
                pltpu.make_async_remote_copy(
                    src_ref=rs.at[LAST * PER + i], dst_ref=lr.at[i - 1], send_sem=sy_send.at[LAST],
                    recv_sem=sy_recv.at[LAST], device_id=chip(i // 2, zoff(2 * LAST + i % 2)),
                    device_id_type=MESH).start()

    def settle_stage(c):
        local_wait(yr.at[c], sy_recv.at[c])
        two = yk[c] + jnp.sum(yr[c].astype(F32), axis=0)
        zs[pl.ds(2 * c, 2)] = two.astype(BF)

        @pl.loop(2 * c, 2 * c + 2)
        def _(p):
            pltpu.make_async_remote_copy(
                src_ref=zs.at[p], dst_ref=zr.at[p], send_sem=sz_send, recv_sem=sz_recv.at[c],
                device_id=chip(0, zoff(p)), device_id_type=MESH).start()

    stores = [
        pltpu.make_async_copy(wout.at[0, pl.ds(0, ff)], dgu_hbm.at[0], o_sem.at[0]),
        pltpu.make_async_copy(wout.at[1, pl.ds(0, ff)], dgu_hbm.at[1], o_sem.at[1]),
        pltpu.make_async_copy(wout.at[2, pl.ds(0, ff)], dd_hbm, o_sem.at[2]),
    ]

    def weight_stage(g):
        h = jnp.concatenate([hid[c, :, g].reshape(fpad, CT) for c in range(CHUNKS)], axis=1)
        wout[g] = jnp.dot(h, rows[g // 2], preferred_element_type=F32).astype(BF)
        for n, store in enumerate(stores):
            pl.when(g == n)(store.start)

    stages = (spread_stage, gather_stage, first_stage, point_stage, second_stage,
              scatter_stage, settle_stage, weight_stage)

    @pl.loop(0, len(ORDER))
    def _(i):
        stage = lookup(0, i)
        c = lookup(1, i)
        for n, run in enumerate(stages):
            pl.when(stage == n)(lambda run=run: run(c))

    acc[...] = yk[LAST, 0]
    for c in range(LAST):
        local_wait(zr.at[pl.ds(2 * c, 2)], sz_recv.at[c])
        acc[...] += zr[2 * c].astype(F32) + zr[2 * c + 1].astype(F32)
    local_wait(lr, sy_recv.at[LAST])
    acc[...] += jnp.sum(lr[...].astype(F32), axis=0)

    out_ref[...] = acc[0:8].astype(BF)
    dtok_ref[...] = acc[8:16].astype(BF)

    local_wait(lr, az_send)
    local_wait(zr, sz_send)
    local_wait(lr, sy_send.at[LAST])

    @pl.loop(0, CHUNKS)
    def _(c):
        local_wait(yr.at[0], ay_send.at[c])

        @pl.when(c < LAST)
        def _():
            local_wait(yr.at[0], sy_send.at[c])

        forward(c).wait_send()
        local_wait(pr.at[c], xr_send.at[c])
        local_wait(pr.at[c], xa_send.at[c])
        exchange(c).wait_send()

    for c in stores:
        c.wait()


def deliver(*refs):
    n = (len(refs) - 2) // 3
    srcs, dsts, bufs = refs[:n], refs[n:2 * n], refs[2 * n:3 * n]
    in_sems, out_sems = refs[3 * n:]
    steps = []
    for a, b, v in zip(srcs, dsts, bufs):
        rows = a.shape[-2]
        cuts = [pl.ds(0, rows)] if rows < 432 else [pl.ds(0, 224), pl.ds(224, rows - 224)]
        for g in range(a.shape[0]) if len(a.shape) == 3 else (None,):
            for cut in cuts:
                at = (cut,) if g is None else (g, cut)
                i = len(steps)
                steps.append((pltpu.make_async_copy(a.at[at], v.at[at], in_sems.at[i]),
                              pltpu.make_async_copy(v.at[at], b.at[at], out_sems.at[i])))
    for load, _ in steps:
        load.start()
    for load, store in steps:
        load.wait()
        store.start()
    for _, store in steps:
        store.wait()


def local(tokens, w_gate_up, w_down, cotangent):
    rows, d = tokens.shape
    ff = w_down.shape[0]
    fpad = -(-ff // (NX * ROWS)) * NX * ROWS
    fq = fpad // NX
    vm = pl.BlockSpec(memory_space=pltpu.VMEM)
    hbm = pl.BlockSpec(memory_space=pl.ANY)
    dma = pltpu.SemaphoreType.DMA
    results = pl.pallas_call(
        kernel,
        out_shape=(
            jax.ShapeDtypeStruct((rows, d), BF),
            jax.ShapeDtypeStruct((rows, d), BF),
            jax.ShapeDtypeStruct((2, ff, d), BF),
            jax.ShapeDtypeStruct((ff, d), BF),
        ),
        in_specs=[vm, vm, hbm, hbm],
        out_specs=(vm, vm, hbm, hbm),
        scratch_shapes=[
            pltpu.VMEM((3, fpad, d), BF),
            pltpu.VMEM((3, fpad, d), BF),
            pltpu.VMEM((CHUNKS, 2, PER, ROWS, d), BF),
            pltpu.VMEM((2, CHUNKS * CT, d), BF),
            pltpu.VMEM((CHUNKS, NX, 3, fq, CT), BF),
            pltpu.VMEM((CHUNKS, NX - 1, 3, fq, CT), BF),
            pltpu.VMEM((CHUNKS, 3, NX, fq, CT), F32),
            pltpu.VMEM((CHUNKS, NX, 3, fq, CT), BF),
            pltpu.VMEM((CHUNKS, 2, CT, d), F32),
            pltpu.VMEM((CHUNKS, 2, HALF, d), F32),
            pltpu.VMEM((CHIPS, ROWS, d), BF),
            pltpu.VMEM((CHUNKS, 2, ROWS, d), F32),
            pltpu.VMEM((CHUNKS - 1, NY - 1, 2, ROWS, d), BF),
            pltpu.VMEM((NZ - 2, ROWS, d), BF),
            pltpu.VMEM((NZ - 2, ROWS, d), BF),
            pltpu.VMEM((PER - 1, ROWS, d), BF),
            pltpu.VMEM((ROWS, d), F32),
            dma((3,)), dma((3,)),
            dma, dma((CHUNKS,)), dma((CHUNKS,)), dma((CHUNKS,)), dma((CHUNKS,)), dma((CHUNKS,)),
            dma((CHUNKS,)), dma((CHUNKS,)), dma((CHUNKS,)), dma((CHUNKS,)),
            dma((CHUNKS,)), dma((CHUNKS,)),
            dma((CHUNKS,)), dma((CHUNKS,)), dma, dma((CHUNKS,)),
        ],
        compiler_params=pltpu.CompilerParams(
            collective_id=0, has_side_effects=True, vmem_limit_bytes=56 * 2**20),
    )(tokens, cotangent, w_gate_up, w_down)
    return pl.pallas_call(
        deliver,
        out_shape=tuple(jax.ShapeDtypeStruct(r.shape, r.dtype) for r in results),
        in_specs=[hbm] * len(results),
        out_specs=(hbm,) * len(results),
        scratch_shapes=[pltpu.VMEM(r.shape, r.dtype) for r in results] + [dma((8,)), dma((8,))],
        compiler_params=pltpu.CompilerParams(vmem_limit_bytes=56 * 2**20),
    )(*results)


def solution(mesh):
    placed = (
        P(("col", "dp"), "row"),
        P(None, ("col", "dp"), "row"),
        P(("col", "dp"), "row"),
        P(("col", "dp"), "row"),
    )
    return jax.shard_map(
        local,
        mesh=mesh,
        in_specs=placed,
        out_specs=(
            P(("col", "dp"), "row"),
            P(("col", "dp"), "row"),
            P(None, ("col", "dp"), "row"),
            P(("col", "dp"), "row"),
        ),
        check_vma=False,
    )
```
